32 devices in a mesh: dp: 4 (over z), row: 4 (over x, core), col: 2 (over y).
Axes of the slice: x: 2, y: 2, z: 4, core: 2. Of those that a mesh axis runs over, the one named last changes fastest.
Arguments:
- tokens: bfloat16 [16384, 1024], P(('dp', 'col'), 'row'), may hold values from -6 to 6
- lengths: int32 [16], P('dp'), may hold values from 128 to 1024, as said below
- qkv_weight: bfloat16 [1024, 3072], P('row', 'col'), may hold values from -0.1875 to 0.1875
- query_bias: float32 [1024], P('col'), may hold values from -4 to 4
- value_bias: float32 [1024], P('col'), may hold values from -0.75 to 0.75
- out_weight: bfloat16 [1024, 1024], P('col', 'row'), may hold values from -2 to 2
- out_bias: float32 [1024], P('row'), may hold values from -4 to 4
- first_norm_scale: float32 [1024], P('row'), may hold values from 0.5 to 1.5
- first_norm_bias: float32 [1024], P('row'), may hold values from -3 to 3
- up_weight: bfloat16 [1024, 4096], P('row', 'col'), may hold values from -0.1875 to 0.1875
- up_bias: float32 [4096], P('col'), may hold values from -4 to 4
- down_weight: bfloat16 [4096, 1024], P('col', 'row'), may hold values from -0.09375 to 0.09375
- down_bias: float32 [1024], P('row'), may hold values from -4 to 4
- second_norm_scale: float32 [1024], P('row'), may hold values from 0.5 to 1.5
- second_norm_bias: float32 [1024], P('row'), may hold values from -3 to 3
- cotangent: bfloat16 [16384, 1024], P(('dp', 'col'), 'row'), may hold values from -6 to 6
Outputs:
- layer_result_output: bfloat16 [16384, 1024], P(('dp', 'col'), 'row')
- grad_tokens: float32 [16384, 1024], P(('dp', 'col'), 'row')
- grad_qkv_weight: float32 [1024, 3072], P('row', 'col')
- grad_query_bias: float32 [1024], P('col')
- grad_value_bias: float32 [1024], P('col')
- grad_out_weight: float32 [1024, 1024], P('col', 'row')
- grad_out_bias: float32 [1024], P('row')
- grad_norm_one_gain: float32 [1024], P('row')
- grad_norm_one_shift: float32 [1024], P('row')
- grad_up_weight: float32 [1024, 4096], P('row', 'col')
- grad_up_bias: float32 [4096], P('col')
- grad_down_weight: float32 [4096, 1024], P('col', 'row')
- grad_down_bias: float32 [1024], P('row')
- grad_norm_two_gain: float32 [1024], P('row')
- grad_norm_two_shift: float32 [1024], P('row')
The draws below stay inside these ranges and needn't reach their ends.
Inputs may be any that keep to these rules, and one draw needn't show every extreme that they name: `lengths`: valid tokens at the start of each sequence; keys at later positions are masked; in every draw some sequence has 1024 and some has 128.
All inputs are finite; a program needn't handle non-finite values.
Results may differ from the reference program's by a relative error of at most 0.012.
The reference program's roundings to bfloat16 on the way count: a program that leaves them out, or rounds other values in their place, can miss the bound.
Values may be sent and summed in bfloat16 or wider, within the bound.
A program may use at most 192 MiB of HBM per device.

```python
import jax
import jax.numpy as jnp
from jax import lax

D = 1024
H = 16
HD = 64
FF = 4096
LENGTH = 1024
SEQS = 16
TOKENS = 16384


def draw_lengths(key, part):
    key = jax.random.fold_in(key, 11)
    key_values, key_first, key_second = jax.random.split(key, 3)
    values = jax.random.randint(key_values, (SEQS,), LENGTH // 8, LENGTH + 1)
    first_pick = jax.random.randint(key_first, (), 0, SEQS)
    second_pick = (first_pick + 1 + jax.random.randint(key_second, (), 0, SEQS - 1)) % SEQS
    values = values.at[first_pick].set(LENGTH).at[second_pick].set(LENGTH // 8)
    return values.astype(jnp.int32)


def level_of(own_key, extent, shards, low, largest):
    def one(position, parts):
        steps = jax.random.uniform(jax.random.fold_in(jax.random.fold_in(own_key, 6), position), (parts,), jnp.float32, low / len(shards), largest / len(shards))
        return jnp.repeat(jnp.exp(steps), extent[position] // parts).reshape((-1,) + (1,) * (len(extent) - position - 1))

    loudness = one(*shards[0])
    for cut in shards[1:]:
        loudness = loudness * one(*cut)
    return loudness


def normal_values(key, extent, deviation, bound, shards=(), kind=jnp.bfloat16):
    level = level_of(key, extent, shards, -0.22, 0.18) if shards else 1.0
    values = jax.random.normal(key, extent, jnp.float32) * deviation * level
    return jnp.minimum(jnp.maximum(values, -bound), bound).astype(kind)


def setup_inputs(seed: int = 0) -> dict:
    arg_keys = jax.random.split(jax.random.key(seed), 17)
    tokens = normal_values(arg_keys[0], (TOKENS, D), 1.0, 6.0, ((0, 8), (1, 4)))
    lengths = draw_lengths(jax.random.fold_in(arg_keys[16], 71), 0)
    qkv_weight = normal_values(arg_keys[2], (D, 3 * D), D ** -0.5, 0.1875, ((0, 4), (1, 2)))
    query_bias = normal_values(arg_keys[3], (D,), 0.3, 4.0, ((0, 2),), jnp.float32)
    value_bias = normal_values(arg_keys[4], (D,), 0.05, 0.75, ((0, 2),), jnp.float32)
    out_weight = normal_values(arg_keys[5], (D, D), 8 ** -0.5, 2.0, ((0, 2), (1, 4)))
    out_bias = normal_values(arg_keys[6], (D,), 0.3, 4.0, ((0, 4),), jnp.float32)
    first_norm_scale = jnp.clip(1.0 + 0.1 * jax.random.normal(arg_keys[7], (D,), jnp.float32), 0.5, 1.5)
    first_norm_bias = normal_values(arg_keys[8], (D,), 0.2, 3.0, ((0, 4),), jnp.float32)
    up_weight = normal_values(arg_keys[9], (D, FF), D ** -0.5, 0.1875, ((0, 4), (1, 2)))
    up_bias = normal_values(arg_keys[10], (FF,), 0.3, 4.0, ((0, 2),), jnp.float32)
    down_weight = normal_values(arg_keys[11], (FF, D), FF ** -0.5, 0.09375, ((0, 2), (1, 4)))
    down_bias = normal_values(arg_keys[12], (D,), 0.3, 4.0, ((0, 4),), jnp.float32)
    second_norm_scale = jnp.clip(1.0 + 0.1 * jax.random.normal(arg_keys[13], (D,), jnp.float32), 0.5, 1.5)
    second_norm_bias = normal_values(arg_keys[14], (D,), 0.2, 3.0, ((0, 4),), jnp.float32)
    cotangent = normal_values(arg_keys[15], (TOKENS, D), 1.0, 6.0, ((0, 8), (1, 4)))
    return dict(tokens=tokens, lengths=lengths, qkv_weight=qkv_weight, query_bias=query_bias, value_bias=value_bias, out_weight=out_weight, out_bias=out_bias, first_norm_scale=first_norm_scale, first_norm_bias=first_norm_bias, up_weight=up_weight, up_bias=up_bias, down_weight=down_weight, down_bias=down_bias, second_norm_scale=second_norm_scale, second_norm_bias=second_norm_bias, cotangent=cotangent)


@jax.custom_vjp
def low(v):
    return lax.optimization_barrier(v.astype(jnp.bfloat16)).astype(jnp.float32)

@jax.custom_vjp
def low_back(v):
    return v

def low_keep(v):
    return (low(v), None)

def low_pass(kept, grad):
    return (grad,)

def back_keep(v):
    return (v, None)

def back_low(kept, grad):
    return (low(grad),)
low.defvjp(low_keep, low_pass)
low_back.defvjp(back_keep, back_low)
norm_epsilon = 1e-12
masked_score = -1e+30
highest_precision = lax.Precision.HIGHEST

def layer_norm(values, gain_vec, shift_vec):
    average = lax.optimization_barrier(jnp.mean(values, axis=-1, keepdims=True))
    centred = values - average
    variance = lax.optimization_barrier(jnp.mean(centred * centred, axis=-1, keepdims=True))
    return centred * lax.rsqrt(variance + norm_epsilon) * gain_vec + shift_vec

def attention(queries, key_part, value_part, length):
    block_rows = min(512, LENGTH)
    visible = (jnp.arange(LENGTH) < length)[None, None, :]

    def one_block(query_block):
        scores = jnp.einsum('qhd,khd->hqk', query_block, key_part, precision=highest_precision) * HD ** (-0.5)
        scores = jnp.where(visible, low_back(scores), masked_score)
        highest = lax.optimization_barrier(jnp.max(scores, axis=2, keepdims=True))
        weights = jnp.exp(scores - highest)
        chances = weights / lax.optimization_barrier(jnp.sum(weights, axis=2, keepdims=True))
        context = jnp.einsum('hqk,khd->qhd', low(chances), value_part, precision=highest_precision)
        return low(low_back(context))
    blocks = queries.reshape(LENGTH // block_rows, block_rows, H, HD)
    return lax.map(jax.checkpoint(one_block), blocks).reshape(LENGTH, H * HD)

def layer(tokens_seq, length, params):
    qkv_weight, query_bias, value_bias, out_weight, out_bias, first_norm_scale, first_norm_bias, up_weight, up_bias, down_weight, down_bias, second_norm_scale, second_norm_bias = params
    head_query = query_bias.reshape(H, HD)
    heads_bias = jnp.stack([head_query, jnp.zeros_like(head_query), value_bias.reshape(H, HD)], axis=1).reshape(3 * D)
    mixed_qkv = jnp.dot(tokens_seq, qkv_weight, precision=highest_precision) + heads_bias
    mixed_qkv = low(low_back(mixed_qkv)).reshape(LENGTH, H, 3, HD)
    context = attention(mixed_qkv[:, :, 0], mixed_qkv[:, :, 1], mixed_qkv[:, :, 2], length)
    first_residual = tokens_seq + low_back(jnp.dot(context, out_weight, precision=highest_precision)) + out_bias
    first_normalized = layer_norm(first_residual, first_norm_scale, first_norm_bias)
    upward = low_back(jnp.dot(low(first_normalized), up_weight, precision=highest_precision) + up_bias)
    hidden = low(jax.nn.gelu(upward, approximate=False))
    second_residual = first_normalized + low_back(jnp.dot(hidden, down_weight, precision=highest_precision)) + down_bias
    return layer_norm(second_residual, second_norm_scale, second_norm_bias)

def reference(tokens, lengths, qkv_weight, query_bias, value_bias, out_weight, out_bias, first_norm_scale, first_norm_bias, up_weight, up_bias, down_weight, down_bias, second_norm_scale, second_norm_bias, cotangent):
    params = (qkv_weight.astype(jnp.float32), query_bias.astype(jnp.float32), value_bias.astype(jnp.float32), out_weight.astype(jnp.float32), out_bias.astype(jnp.float32), first_norm_scale.astype(jnp.float32), first_norm_bias.astype(jnp.float32), up_weight.astype(jnp.float32), up_bias.astype(jnp.float32), down_weight.astype(jnp.float32), down_bias.astype(jnp.float32), second_norm_scale.astype(jnp.float32), second_norm_bias.astype(jnp.float32))
    inputs = tokens.astype(jnp.float32).reshape(SEQS, LENGTH, D)
    grads_in = cotangent.astype(jnp.float32).reshape(SEQS, LENGTH, D)

    def one_sequence(totals, sequence_in):
        tokens_seq, grad_seq, length = sequence_in
        outputs, pullback = jax.vjp(lambda values, weights: layer(values, length, weights), tokens_seq, params)
        grad_values, grad_params = pullback(grad_seq)
        totals = jax.tree.map(lambda former, latter: former + latter, totals, grad_params)
        return (totals, (outputs, grad_values))
    zero_grads = jax.tree.map(jnp.zeros_like, params)
    grad_sums, (outputs, grad_values) = lax.scan(one_sequence, zero_grads, (inputs, grads_in, lengths))
    return (outputs.reshape(TOKENS, D).astype(jnp.bfloat16), grad_values.reshape(TOKENS, D), grad_sums[0], grad_sums[1], grad_sums[2], grad_sums[3], grad_sums[4], grad_sums[5], grad_sums[6], grad_sums[7], grad_sums[8], grad_sums[9], grad_sums[10], grad_sums[11], grad_sums[12])
```

```python
import jax
import jax.numpy as jnp
from jax import lax
from jax.experimental import pallas as pl
from jax.experimental.pallas import tpu as pltpu
from jax.sharding import Mesh, PartitionSpec as P

HD = 64
LENGTH = 1024
QUERY_BLOCK = 256

norm_epsilon = 1e-12
masked_score = -1e30
F32 = jnp.float32
BF16 = jnp.bfloat16


def swap(values, axis):
    return lax.ppermute(values, axis, [(0, 1), (1, 0)])


def pick(values, index, amount):
    return lax.dynamic_slice_in_dim(values, index * amount, amount, 0)


def in_order(index, mine, other, axis=0):
    return jnp.where(
        index == 0,
        jnp.concatenate([mine, other], axis=axis),
        jnp.concatenate([other, mine], axis=axis),
    )


def dot(left, right, contract=((1,), (0,))):
    return lax.dot_general(left, right, (contract, ((), ())), preferred_element_type=F32)


def gather_plane(first, second):
    first_x = swap(first, "x")
    second_y = swap(second, "col")
    first_y = swap(first, "col")
    second_x = swap(second, "x")
    first_xy = swap(first_x, "col")
    second_xy = swap(second_y, "x")
    return (
        [[first, first_y], [first_x, first_xy]],
        [[second, second_y], [second_x, second_xy]],
    )


def scatter_plane(first, second):
    def go(blocks, axes):
        near = blocks[0][0].astype(F32) + swap(blocks[0][1], axes[0]).astype(F32)
        far = blocks[1][0].astype(F32) + swap(blocks[1][1], axes[0]).astype(F32)
        return near + swap(far.astype(BF16), axes[1]).astype(F32)

    turned = [[second[0][0], second[1][0]], [second[0][1], second[1][1]]]
    return go(first, ("col", "x")), go(turned, ("x", "col"))


def over_groups(values, after):
    values = tuple(value.astype(BF16) for value in values)
    if after is not None:
        values, after = lax.optimization_barrier((values, after))
    return lax.psum(values, "dp")


def gather_core(values):
    return jnp.concatenate([values, swap(values, "core")], axis=0)


def reduce_core(partials):
    half = partials.shape[0] // 2
    return partials[:half] + swap(partials[half:], "core")


def attend_body(place_ref, mixed_ref, context_ref, sums_ref):
    length = place_ref[0]
    offset = place_ref[1]
    count = mixed_ref.shape[0]
    position = lax.broadcasted_iota(jnp.int32, (count, 1), 0) + offset
    position = jnp.where(position >= count, position - count, position)
    visible = position < length
    for block in range(count // QUERY_BLOCK):
        rows = pl.ds(block * QUERY_BLOCK, QUERY_BLOCK)
        parts = []
        for head in range(2):
            start = head * 3 * HD
            query = mixed_ref[rows, start : start + HD] * jnp.asarray(HD ** (-0.5), BF16)
            key = mixed_ref[:, start + HD : start + 2 * HD]
            value = mixed_ref[:, start + 2 * HD : start + 3 * HD]
            scores = jnp.where(visible, dot(key, query, ((1,), (1,))), masked_score)
            highest = jnp.max(scores, axis=0, keepdims=True)
            weights = jnp.exp(scores - highest)
            totals = jnp.sum(weights, axis=0, keepdims=True)
            chances = (weights * (1.0 / totals)).astype(BF16)
            parts.append(dot(value, chances, ((0,), (0,))))
            sums_ref[0, head : head + 1, rows] = highest + jnp.log(totals)
        context_ref[rows, :] = jnp.concatenate(parts, axis=0).T.astype(BF16)


def attend(mixed, place):
    count = mixed.shape[0]
    pairs = mixed.shape[1] // (6 * HD)
    return pl.pallas_call(
        attend_body,
        grid=(pairs,),
        in_specs=[
            pl.BlockSpec(memory_space=pltpu.SMEM),
            pl.BlockSpec((count, 6 * HD), lambda pair: (0, pair)),
        ],
        out_specs=[
            pl.BlockSpec((count, 2 * HD), lambda pair: (0, pair)),
            pl.BlockSpec((1, 2, count), lambda pair: (pair, 0, 0)),
        ],
        out_shape=[
            jax.ShapeDtypeStruct((count, pairs * 2 * HD), BF16),
            jax.ShapeDtypeStruct((pairs, 2, count), F32),
        ],
        compiler_params=pltpu.CompilerParams(vmem_limit_bytes=40 * 2**20),
        cost_estimate=pl.CostEstimate(
            flops=pairs * 8 * count * count * HD,
            bytes_accessed=mixed.size * 3,
            transcendentals=pairs * 2 * count * count,
        ),
        name="attend",
    )(place, mixed)


def attend_back_body(place_ref, mixed_ref, grad_ref, sums_ref, out_ref):
    length = place_ref[0]
    offset = place_ref[1]
    count = mixed_ref.shape[0]
    position = lax.broadcasted_iota(jnp.int32, (count, 1), 0) + offset
    position = jnp.where(position >= count, position - count, position)
    visible = position < length
    scale = HD ** (-0.5)
    for head in range(2):
        start = head * 3 * HD
        key = mixed_ref[:, start + HD : start + 2 * HD]
        value = mixed_ref[:, start + 2 * HD : start + 3 * HD]
        grad_key = jnp.zeros((count, HD), F32)
        grad_value = jnp.zeros((count, HD), F32)
        for block in range(count // QUERY_BLOCK):
            rows = pl.ds(block * QUERY_BLOCK, QUERY_BLOCK)
            query = mixed_ref[rows, start : start + HD] * jnp.asarray(scale, BF16)
            grad = grad_ref[rows, head * HD : (head + 1) * HD]
            scores = jnp.where(visible, dot(key, query, ((1,), (1,))), masked_score)
            chances = jnp.exp(scores - sums_ref[0, head : head + 1, rows])
            grad_chances = dot(value, grad, ((1,), (1,)))
            inner = jnp.sum(chances * grad_chances, axis=0, keepdims=True)
            grad_scores = (chances * (grad_chances - inner)).astype(BF16)
            grad_value += dot(chances.astype(BF16), grad)
            grad_key += dot(grad_scores, query)
            grad_query = dot(key, grad_scores, ((0,), (0,))) * scale
            out_ref[rows, start : start + HD] = grad_query.T.astype(BF16)
        out_ref[:, start + HD : start + 2 * HD] = grad_key.astype(BF16)
        out_ref[:, start + 2 * HD : start + 3 * HD] = grad_value.astype(BF16)


def attend_back(mixed, grad_context, log_sums, place):
    count = mixed.shape[0]
    pairs = mixed.shape[1] // (6 * HD)
    return pl.pallas_call(
        attend_back_body,
        grid=(pairs,),
        in_specs=[
            pl.BlockSpec(memory_space=pltpu.SMEM),
            pl.BlockSpec((count, 6 * HD), lambda pair: (0, pair)),
            pl.BlockSpec((count, 2 * HD), lambda pair: (0, pair)),
            pl.BlockSpec((1, 2, count), lambda pair: (pair, 0, 0)),
        ],
        out_specs=pl.BlockSpec((count, 6 * HD), lambda pair: (0, pair)),
        out_shape=jax.ShapeDtypeStruct(mixed.shape, BF16),
        compiler_params=pltpu.CompilerParams(vmem_limit_bytes=40 * 2**20),
        cost_estimate=pl.CostEstimate(
            flops=pairs * 20 * count * count * HD,
            bytes_accessed=mixed.size * 5,
            transcendentals=pairs * 2 * count * count,
        ),
        name="attend_back",
    )(place, mixed, grad_context, log_sums)


def normalize(values, gain_vec, shift_vec):
    average = jnp.mean(values, axis=1, keepdims=True)
    centred = values - average
    variance = jnp.mean(centred * centred, axis=1, keepdims=True)
    inverse = lax.rsqrt(variance + norm_epsilon)
    normed = centred * inverse
    return normed * gain_vec + shift_vec, normed, inverse


def normalize_back(grad_out, normed, inverse, gain_vec):
    scaled = grad_out * gain_vec
    grad_in = inverse * (
        scaled
        - jnp.mean(scaled, axis=1, keepdims=True)
        - normed * jnp.mean(scaled * normed, axis=1, keepdims=True)
    )
    return grad_in, jnp.sum(grad_out * normed, axis=0), jnp.sum(grad_out, axis=0)


def shards(
    tokens,
    lengths,
    qkv_weight,
    query_bias,
    value_bias,
    out_weight,
    out_bias,
    first_norm_scale,
    first_norm_bias,
    up_weight,
    up_bias,
    down_weight,
    down_bias,
    second_norm_scale,
    second_norm_bias,
    cotangent,
):
    x = lax.axis_index("x")
    core = lax.axis_index("core")
    col = lax.axis_index("col")
    width = tokens.shape[1]
    half = LENGTH // 2
    place = jnp.stack(
        [lax.dynamic_index_in_dim(lengths, 2 * col + x, 0, False), core * half]
    ).astype(jnp.int32)

    def by_core(mine, other):
        return jnp.where(core == 0, mine, other), jnp.where(core == 0, other, mine)

    def pair_columns(values):
        mine = pick(values, x, LENGTH)
        other = swap(pick(values, 1 - x, LENGTH), "x")
        return jnp.concatenate([mine, other], axis=1)

    def spread(parts):
        mine, other = by_core(*parts)
        return jnp.concatenate(
            [
                mine[:, :width],
                other[:, :width],
                mine[:, width:],
                other[:, width:],
            ],
            axis=1,
        )

    token_pair = pair_columns(tokens)
    token_pair = jnp.concatenate(
        [pick(token_pair, core, half), pick(token_pair, 1 - core, half)], axis=0
    )
    came = swap(token_pair, "core")
    came = jnp.concatenate([came[half:], came[:half]], axis=0)
    tokens_all = spread((token_pair, came))

    def column_share(weight):
        amount = weight.shape[1] // 2
        mine = lax.dynamic_slice_in_dim(weight, core * amount, amount, 1)
        other = swap(lax.dynamic_slice_in_dim(weight, (1 - core) * amount, amount, 1), "core")
        return by_core(mine, other)

    def row_share(weight):
        amount = weight.shape[0] // 2
        return by_core(
            pick(weight, core, amount), swap(pick(weight, 1 - core, amount), "core")
        )

    def full_rows(halves):
        first, second = halves
        return jnp.concatenate(
            [
                jnp.concatenate(blocks, axis=1)
                for blocks in (first[0], second[0], first[1], second[1])
            ],
            axis=0,
        )

    def full_columns(halves):
        first, second = halves
        return jnp.concatenate(
            [
                jnp.concatenate(
                    [first[0][side], second[0][side], first[1][side], second[1][side]], axis=1
                )
                for side in range(2)
            ],
            axis=0,
        )

    qkv_full = full_rows(gather_plane(*column_share(qkv_weight)))
    out_full = full_columns(gather_plane(*row_share(out_weight)))
    up_full = full_rows(gather_plane(*column_share(up_weight)))
    down_full = full_columns(gather_plane(*row_share(down_weight)))

    row_vectors = lax.all_gather(
        jnp.stack(
            [
                out_bias,
                first_norm_scale,
                first_norm_bias,
                down_bias,
                second_norm_scale,
                second_norm_bias,
            ]
        ),
        ("x", "core"),
        axis=0,
    )
    count = row_vectors.shape[1]

    def turn(blocks, axis_index, axis):
        return jnp.where(axis_index == 0, blocks, jnp.flip(blocks, axis))

    row_vectors = row_vectors.reshape(2, 2, count, width)
    row_vectors = turn(row_vectors, x, 0)
    row_vectors = row_vectors.transpose(2, 0, 1, 3).reshape(count, 4 * width)
    out_bias_all, gain_one, shift_one, down_bias_all, gain_two, shift_two = [
        row_vectors[index] for index in range(count)
    ]
    head_amount = query_bias.shape[0]
    up_amount = up_bias.shape[0]
    col_vectors = lax.all_gather(
        jnp.concatenate([query_bias, value_bias, up_bias]), "col", axis=0
    )
    col_vectors = turn(col_vectors, col, 0)

    def core_columns(values):
        amount = values.shape[1] // 2
        return lax.dynamic_slice_in_dim(values, core * amount, amount, 1)

    query_bias_here = core_columns(col_vectors[:, :head_amount]).reshape(-1, HD)
    value_bias_here = core_columns(col_vectors[:, head_amount : 2 * head_amount]).reshape(-1, HD)
    up_bias_here = core_columns(col_vectors[:, 2 * head_amount :]).reshape(-1)
    heads_bias = jnp.stack(
        [query_bias_here, jnp.zeros_like(query_bias_here), value_bias_here], axis=1
    ).reshape(-1)

    mixed = (dot(tokens_all, qkv_full) + heads_bias).astype(BF16)
    context, log_sums = attend(mixed, place)
    tokens_here = tokens_all[:half].astype(F32)
    first_residual = tokens_here + reduce_core(dot(context, out_full)) + out_bias_all
    first_normalized, first_standardized, first_inverse = normalize(
        first_residual, gain_one, shift_one
    )
    normed_all = gather_core(first_normalized.astype(BF16))
    upward = dot(normed_all, up_full) + up_bias_here
    hidden_f, gelu_pull = jax.vjp(
        lambda values: jax.nn.gelu(values, approximate=False), upward
    )
    hidden = hidden_f.astype(BF16)
    second_residual = first_normalized + reduce_core(dot(hidden, down_full)) + down_bias_all
    layer_result, second_standardized, second_inverse = normalize(
        second_residual, gain_two, shift_two
    )

    def hand_back(values):
        kept, sent = by_core(
            jnp.concatenate([values[:, :width], values[:, 2 * width : 3 * width]], axis=1),
            jnp.concatenate([values[:, width : 2 * width], values[:, 3 * width :]], axis=1),
        )
        whole = in_order(core, kept, swap(sent, "core"))
        mine = whole[:, :width]
        other = swap(whole[:, width:].astype(BF16), "x").astype(values.dtype)
        return in_order(x, mine, other)

    layer_result_output = hand_back(layer_result.astype(BF16))

    grad_pair = pair_columns(cotangent)
    cotangent_here = spread(
        (pick(grad_pair, core, half), swap(pick(grad_pair, 1 - core, half), "core"))
    ).astype(F32)
    grad_resid_two, grad_gain_two, grad_shift_two = normalize_back(
        cotangent_here, second_standardized, second_inverse, gain_two
    )
    grad_down_bias = jnp.sum(grad_resid_two, axis=0)
    grad_down_all = gather_core(grad_resid_two.astype(BF16))

    def row_blocks(grad):
        amount = grad.shape[1] // 2
        sides = [
            [grad[r * width : (r + 1) * width, s * amount : (s + 1) * amount] for s in range(2)]
            for r in range(4)
        ]
        return [sides[0], sides[2]], [sides[1], sides[3]]

    def column_blocks(grad):
        amount = grad.shape[0] // 2
        sides = [
            [grad[s * amount : (s + 1) * amount, r * width : (r + 1) * width] for s in range(2)]
            for r in range(4)
        ]
        return [sides[0], sides[2]], [sides[1], sides[3]]

    def settle(grad, blocks, axis, after):
        first, second = over_groups(scatter_plane(*blocks(grad.astype(BF16))), after)
        mine, other = by_core(first, second)
        return in_order(core, mine, swap(other, "core"), axis).astype(F32), (first, second)

    across = ((0,), (0,))
    turned = ((1,), (1,))
    grad_down_weight, done = settle(
        dot(hidden, grad_down_all, across), column_blocks, 0, None
    )
    (grad_upward,) = gelu_pull(dot(grad_down_all, down_full, turned))
    grad_upward = grad_upward.astype(BF16)
    grad_up_bias = jnp.sum(grad_upward, axis=0, dtype=F32)
    grad_up_weight, done = settle(dot(normed_all, grad_upward, across), row_blocks, 1, done)
    grad_normalized = grad_resid_two + reduce_core(dot(grad_upward, up_full, turned))
    grad_resid_one, grad_gain_one, grad_shift_one = normalize_back(
        grad_normalized, first_standardized, first_inverse, gain_one
    )
    grad_out_bias = jnp.sum(grad_resid_one, axis=0)
    grad_attn_all = gather_core(grad_resid_one.astype(BF16))
    grad_out_weight, done = settle(
        dot(context, grad_attn_all, across), column_blocks, 0, done
    )
    grad_context = dot(grad_attn_all, out_full, turned).astype(BF16)
    grad_mixed = attend_back(mixed, grad_context, log_sums, place)
    grad_qkv_weight, done = settle(dot(tokens_all, grad_mixed, across), row_blocks, 1, done)
    grad_tokens = hand_back(grad_resid_one + reduce_core(dot(grad_mixed, qkv_full, turned)))

    def row_wide(values):
        blocks = values.reshape(2, 2, width)
        return turn(blocks, x, 0).reshape(-1)

    def col_wide(values):
        blocks = values.reshape(2, 1, -1)
        blocks = turn(blocks, col, 0)
        zeros = jnp.zeros_like(blocks)
        return in_order(core, blocks, zeros, 1).reshape(-1)

    everywhere = ("dp", "x", "core", "col")
    row_list = [
        grad_out_bias,
        grad_gain_one,
        grad_shift_one,
        grad_down_bias,
        grad_gain_two,
        grad_shift_two,
    ]
    early = lax.psum(
        jnp.concatenate([row_wide(values) for values in row_list] + [col_wide(grad_up_bias)]),
        everywhere,
    )
    row_sums = [
        lax.dynamic_slice_in_dim(
            early, index * 4 * width + (2 * x + core) * width, width, 0
        )
        for index in range(count)
    ]
    up_sum = lax.dynamic_slice_in_dim(early, count * 4 * width + col * up_amount, up_amount, 0)
    head_sums = jnp.sum(grad_mixed, axis=0, dtype=F32).reshape(-1, 3, HD)
    late = lax.psum(
        jnp.stack([col_wide(head_sums[:, 0].reshape(-1)), col_wide(head_sums[:, 2].reshape(-1))]),
        everywhere,
    )
    late = lax.dynamic_slice_in_dim(late, col * head_amount, head_amount, 1)
    return (
        layer_result_output,
        grad_tokens,
        grad_qkv_weight,
        late[0],
        late[1],
        grad_out_weight,
        row_sums[0],
        row_sums[1],
        row_sums[2],
        grad_up_weight,
        up_sum,
        grad_down_weight,
        row_sums[3],
        row_sums[4],
        row_sums[5],
    )


def solution(mesh):
    sizes = mesh.shape
    fine = Mesh(
        mesh.devices.reshape(sizes["dp"], sizes["row"] // 2, 2, sizes["col"]),
        ("dp", "x", "core", "col"),
    )
    row = ("x", "core")
    activation = P(("dp", "col"), row)
    return jax.shard_map(
        shards,
        mesh=fine,
        in_specs=(
            activation,
            P("dp"),
            P(row, "col"),
            P("col"),
            P("col"),
            P("col", row),
            P(row),
            P(row),
            P(row),
            P(row, "col"),
            P("col"),
            P("col", row),
            P(row),
            P(row),
            P(row),
            activation,
        ),
        out_specs=(
            activation,
            activation,
            P(row, "col"),
            P("col"),
            P("col"),
            P("col", row),
            P(row),
            P(row),
            P(row),
            P(row, "col"),
            P("col"),
            P("col", row),
            P(row),
            P(row),
            P(row),
        ),
        check_vma=False,
    )
```

```python
import jax
import jax.numpy as jnp
from jax import lax
from jax.experimental import pallas as pl
from jax.experimental.pallas import tpu as pltpu
from jax.sharding import Mesh, PartitionSpec as P

HD = 64
LENGTH = 1024
QUERY_BLOCK = 256

norm_epsilon = 1e-12
masked_score = -1e30
F32 = jnp.float32
BF16 = jnp.bfloat16


def swap(values, axis):
    return lax.ppermute(values, axis, [(0, 1), (1, 0)])


def pick(values, index, amount):
    return lax.dynamic_slice_in_dim(values, index * amount, amount, 0)


def in_order(index, mine, other, axis=0):
    return jnp.where(
        index == 0,
        jnp.concatenate([mine, other], axis=axis),
        jnp.concatenate([other, mine], axis=axis),
    )


def dot(left, right, contract=((1,), (0,))):
    return lax.dot_general(left, right, (contract, ((), ())), preferred_element_type=F32)


def gather_plane(first, second):
    first_x = swap(first, "x")
    second_y = swap(second, "col")
    first_y = swap(first, "col")
    second_x = swap(second, "x")
    first_xy = swap(first_x, "col")
    second_xy = swap(second_y, "x")
    return (
        [[first, first_y], [first_x, first_xy]],
        [[second, second_y], [second_x, second_xy]],
    )


def scatter_plane(first, second):
    def go(blocks, axes):
        near = blocks[0][0].astype(F32) + swap(blocks[0][1], axes[0]).astype(F32)
        far = blocks[1][0].astype(F32) + swap(blocks[1][1], axes[0]).astype(F32)
        return near + swap(far.astype(BF16), axes[1]).astype(F32)

    turned = [[second[0][0], second[1][0]], [second[0][1], second[1][1]]]
    return go(first, ("col", "x")), go(turned, ("x", "col"))


def over_groups(values, after):
    values = tuple(value.astype(BF16) for value in values)
    if after is not None:
        values, after = lax.optimization_barrier((values, after))
    return lax.psum(values, "dp")


def gather_core(values):
    return jnp.concatenate([values, swap(values, "core")], axis=0)


def reduce_core(partials):
    half = partials.shape[0] // 2
    return partials[:half] + swap(partials[half:], "core")


def attend_body(place_ref, mixed_ref, context_ref, sums_ref):
    length = place_ref[0]
    offset = place_ref[1]
    count = mixed_ref.shape[0]
    position = lax.broadcasted_iota(jnp.int32, (count, 1), 0) + offset
    position = jnp.where(position >= count, position - count, position)
    visible = position < length
    for block in range(count // QUERY_BLOCK):
        rows = pl.ds(block * QUERY_BLOCK, QUERY_BLOCK)
        parts = []
        for head in range(2):
            start = head * 3 * HD
            query = mixed_ref[rows, start : start + HD] * jnp.asarray(HD ** (-0.5), BF16)
            key = mixed_ref[:, start + HD : start + 2 * HD]
            value = mixed_ref[:, start + 2 * HD : start + 3 * HD]
            scores = jnp.where(visible, dot(key, query, ((1,), (1,))), masked_score)
            highest = jnp.max(scores, axis=0, keepdims=True)
            weights = jnp.exp(scores - highest)
            totals = jnp.sum(weights, axis=0, keepdims=True)
            chances = (weights * (1.0 / totals)).astype(BF16)
            parts.append(dot(value, chances, ((0,), (0,))))
            sums_ref[0, head : head + 1, rows] = highest + jnp.log(totals)
        context_ref[rows, :] = jnp.concatenate(parts, axis=0).T.astype(BF16)


def attend(mixed, place):
    count = mixed.shape[0]
    pairs = mixed.shape[1] // (6 * HD)
    return pl.pallas_call(
        attend_body,
        grid=(pairs,),
        in_specs=[
            pl.BlockSpec(memory_space=pltpu.SMEM),
            pl.BlockSpec((count, 6 * HD), lambda pair: (0, pair)),
        ],
        out_specs=[
            pl.BlockSpec((count, 2 * HD), lambda pair: (0, pair)),
            pl.BlockSpec((1, 2, count), lambda pair: (pair, 0, 0)),
        ],
        out_shape=[
            jax.ShapeDtypeStruct((count, pairs * 2 * HD), BF16),
            jax.ShapeDtypeStruct((pairs, 2, count), F32),
        ],
        compiler_params=pltpu.CompilerParams(vmem_limit_bytes=40 * 2**20),
        cost_estimate=pl.CostEstimate(
            flops=pairs * 8 * count * count * HD,
            bytes_accessed=mixed.size * 3,
            transcendentals=pairs * 2 * count * count,
        ),
        name="attend",
    )(place, mixed)


def attend_back_body(place_ref, mixed_ref, grad_ref, sums_ref, out_ref):
    length = place_ref[0]
    offset = place_ref[1]
    count = mixed_ref.shape[0]
    position = lax.broadcasted_iota(jnp.int32, (count, 1), 0) + offset
    position = jnp.where(position >= count, position - count, position)
    visible = position < length
    scale = HD ** (-0.5)
    for head in range(2):
        start = head * 3 * HD
        key = mixed_ref[:, start + HD : start + 2 * HD]
        value = mixed_ref[:, start + 2 * HD : start + 3 * HD]
        grad_key = jnp.zeros((count, HD), F32)
        grad_value = jnp.zeros((count, HD), F32)
        for block in range(count // QUERY_BLOCK):
            rows = pl.ds(block * QUERY_BLOCK, QUERY_BLOCK)
            query = mixed_ref[rows, start : start + HD] * jnp.asarray(scale, BF16)
            grad = grad_ref[rows, head * HD : (head + 1) * HD]
            scores = jnp.where(visible, dot(key, query, ((1,), (1,))), masked_score)
            chances = jnp.exp(scores - sums_ref[0, head : head + 1, rows])
            grad_chances = dot(value, grad, ((1,), (1,)))
            inner = jnp.sum(chances * grad_chances, axis=0, keepdims=True)
            grad_scores = (chances * (grad_chances - inner)).astype(BF16)
            grad_value += dot(chances.astype(BF16), grad)
            grad_key += dot(grad_scores, query)
            grad_query = dot(key, grad_scores, ((0,), (0,))) * scale
            out_ref[rows, start : start + HD] = grad_query.T.astype(BF16)
        out_ref[:, start + HD : start + 2 * HD] = grad_key.astype(BF16)
        out_ref[:, start + 2 * HD : start + 3 * HD] = grad_value.astype(BF16)


def attend_back(mixed, grad_context, log_sums, place):
    count = mixed.shape[0]
    pairs = mixed.shape[1] // (6 * HD)
    return pl.pallas_call(
        attend_back_body,
        grid=(pairs,),
        in_specs=[
            pl.BlockSpec(memory_space=pltpu.SMEM),
            pl.BlockSpec((count, 6 * HD), lambda pair: (0, pair)),
            pl.BlockSpec((count, 2 * HD), lambda pair: (0, pair)),
            pl.BlockSpec((1, 2, count), lambda pair: (pair, 0, 0)),
        ],
        out_specs=pl.BlockSpec((count, 6 * HD), lambda pair: (0, pair)),
        out_shape=jax.ShapeDtypeStruct(mixed.shape, BF16),
        compiler_params=pltpu.CompilerParams(vmem_limit_bytes=40 * 2**20),
        cost_estimate=pl.CostEstimate(
            flops=pairs * 20 * count * count * HD,
            bytes_accessed=mixed.size * 5,
            transcendentals=pairs * 2 * count * count,
        ),
        name="attend_back",
    )(place, mixed, grad_context, log_sums)


def normalize(values, gain_vec, shift_vec):
    average = jnp.mean(values, axis=1, keepdims=True)
    centred = values - average
    variance = jnp.mean(centred * centred, axis=1, keepdims=True)
    inverse = lax.rsqrt(variance + norm_epsilon)
    normed = centred * inverse
    return normed * gain_vec + shift_vec, normed, inverse


def normalize_back(grad_out, normed, inverse, gain_vec):
    scaled = grad_out * gain_vec
    grad_in = inverse * (
        scaled
        - jnp.mean(scaled, axis=1, keepdims=True)
        - normed * jnp.mean(scaled * normed, axis=1, keepdims=True)
    )
    return grad_in, jnp.sum(grad_out * normed, axis=0), jnp.sum(grad_out, axis=0)


def shards(
    tokens,
    lengths,
    qkv_weight,
    query_bias,
    value_bias,
    out_weight,
    out_bias,
    first_norm_scale,
    first_norm_bias,
    up_weight,
    up_bias,
    down_weight,
    down_bias,
    second_norm_scale,
    second_norm_bias,
    cotangent,
):
    x = lax.axis_index("x")
    core = lax.axis_index("core")
    col = lax.axis_index("col")
    width = tokens.shape[1]
    half = LENGTH // 2
    place = jnp.stack(
        [lax.dynamic_index_in_dim(lengths, 2 * col + x, 0, False), core * half]
    ).astype(jnp.int32)

    def by_core(mine, other):
        return jnp.where(core == 0, mine, other), jnp.where(core == 0, other, mine)

    def pair_columns(values):
        mine = pick(values, x, LENGTH)
        other = swap(pick(values, 1 - x, LENGTH), "x")
        return jnp.concatenate([mine, other], axis=1)

    def spread(parts):
        mine, other = by_core(*parts)
        return jnp.concatenate(
            [
                mine[:, :width],
                other[:, :width],
                mine[:, width:],
                other[:, width:],
            ],
            axis=1,
        )

    token_pair = pair_columns(tokens)
    token_pair = jnp.concatenate(
        [pick(token_pair, core, half), pick(token_pair, 1 - core, half)], axis=0
    )
    came = swap(token_pair, "core")
    came = jnp.concatenate([came[half:], came[:half]], axis=0)
    tokens_all = spread((token_pair, came))

    def column_share(weight):
        amount = weight.shape[1] // 2
        mine = lax.dynamic_slice_in_dim(weight, core * amount, amount, 1)
        other = swap(lax.dynamic_slice_in_dim(weight, (1 - core) * amount, amount, 1), "core")
        return by_core(mine, other)

    def row_share(weight):
        amount = weight.shape[0] // 2
        return by_core(
            pick(weight, core, amount), swap(pick(weight, 1 - core, amount), "core")
        )

    def full_rows(halves):
        first, second = halves
        return jnp.concatenate(
            [
                jnp.concatenate(blocks, axis=1)
                for blocks in (first[0], second[0], first[1], second[1])
            ],
            axis=0,
        )

    def full_columns(halves):
        first, second = halves
        return jnp.concatenate(
            [
                jnp.concatenate(
                    [first[0][side], second[0][side], first[1][side], second[1][side]], axis=1
                )
                for side in range(2)
            ],
            axis=0,
        )

    qkv_full = full_rows(gather_plane(*column_share(qkv_weight)))
    out_full = full_columns(gather_plane(*row_share(out_weight)))
    up_full = full_rows(gather_plane(*column_share(up_weight)))
    down_full = full_columns(gather_plane(*row_share(down_weight)))

    row_vectors = lax.all_gather(
        jnp.stack(
            [
                out_bias,
                first_norm_scale,
                first_norm_bias,
                down_bias,
                second_norm_scale,
                second_norm_bias,
            ]
        ),
        ("x", "core"),
        axis=0,
    )
    count = row_vectors.shape[1]

    def turn(blocks, axis_index, axis):
        return jnp.where(axis_index == 0, blocks, jnp.flip(blocks, axis))

    row_vectors = row_vectors.reshape(2, 2, count, width)
    row_vectors = turn(row_vectors, x, 0)
    row_vectors = row_vectors.transpose(2, 0, 1, 3).reshape(count, 4 * width)
    out_bias_all, gain_one, shift_one, down_bias_all, gain_two, shift_two = [
        row_vectors[index] for index in range(count)
    ]
    head_amount = query_bias.shape[0]
    up_amount = up_bias.shape[0]
    col_vectors = lax.all_gather(
        jnp.concatenate([query_bias, value_bias, up_bias]), "col", axis=0
    )
    col_vectors = turn(col_vectors, col, 0)

    def core_columns(values):
        amount = values.shape[1] // 2
        return lax.dynamic_slice_in_dim(values, core * amount, amount, 1)

    query_bias_here = core_columns(col_vectors[:, :head_amount]).reshape(-1, HD)
    value_bias_here = core_columns(col_vectors[:, head_amount : 2 * head_amount]).reshape(-1, HD)
    up_bias_here = core_columns(col_vectors[:, 2 * head_amount :]).reshape(-1)
    heads_bias = jnp.stack(
        [query_bias_here, jnp.zeros_like(query_bias_here), value_bias_here], axis=1
    ).reshape(-1)

    mixed = (dot(tokens_all, qkv_full) + heads_bias).astype(BF16)
    context, log_sums = attend(mixed, place)
    tokens_here = tokens_all[:half].astype(F32)
    first_residual = tokens_here + reduce_core(dot(context, out_full)) + out_bias_all
    first_normalized, first_standardized, first_inverse = normalize(
        first_residual, gain_one, shift_one
    )
    normed_all = gather_core(first_normalized.astype(BF16))
    upward = dot(normed_all, up_full) + up_bias_here
    portion = 0.5 * (1.0 + lax.erf(upward * (0.5**0.5)))
    slope = portion + upward * (jnp.exp(-0.5 * upward * upward) * (0.5 / jnp.pi) ** 0.5)
    hidden = (upward * portion).astype(BF16)
    second_residual = first_normalized + reduce_core(dot(hidden, down_full)) + down_bias_all
    layer_result, second_standardized, second_inverse = normalize(
        second_residual, gain_two, shift_two
    )

    def hand_back(values):
        kept, sent = by_core(
            jnp.concatenate([values[:, :width], values[:, 2 * width : 3 * width]], axis=1),
            jnp.concatenate([values[:, width : 2 * width], values[:, 3 * width :]], axis=1),
        )
        whole = in_order(core, kept, swap(sent, "core"))
        mine = whole[:, :width]
        other = swap(whole[:, width:].astype(BF16), "x").astype(values.dtype)
        return in_order(x, mine, other)

    layer_result_output = hand_back(layer_result.astype(BF16))

    grad_pair = pair_columns(cotangent)
    cotangent_here = spread(
        (pick(grad_pair, core, half), swap(pick(grad_pair, 1 - core, half), "core"))
    ).astype(F32)
    grad_resid_two, grad_gain_two, grad_shift_two = normalize_back(
        cotangent_here, second_standardized, second_inverse, gain_two
    )
    grad_down_bias = jnp.sum(grad_resid_two, axis=0)
    grad_down_all = gather_core(grad_resid_two.astype(BF16))

    def row_blocks(grad):
        amount = grad.shape[1] // 2
        sides = [
            [grad[r * width : (r + 1) * width, s * amount : (s + 1) * amount] for s in range(2)]
            for r in range(4)
        ]
        return [sides[0], sides[2]], [sides[1], sides[3]]

    def column_blocks(grad):
        amount = grad.shape[0] // 2
        sides = [
            [grad[s * amount : (s + 1) * amount, r * width : (r + 1) * width] for s in range(2)]
            for r in range(4)
        ]
        return [sides[0], sides[2]], [sides[1], sides[3]]

    def plane_sums(grad, blocks):
        return scatter_plane(*blocks(grad.astype(BF16)))

    def settle(first, second, axis):
        mine, other = by_core(first, second)
        return in_order(core, mine, swap(other, "core"), axis).astype(F32)

    across = ((0,), (0,))
    turned = ((1,), (1,))
    down_sums = plane_sums(dot(hidden, grad_down_all, across), column_blocks)
    grad_upward = (dot(grad_down_all, down_full, turned) * slope).astype(BF16)
    grad_up_bias = jnp.sum(grad_upward, axis=0, dtype=F32)
    up_sums = plane_sums(dot(normed_all, grad_upward, across), row_blocks)
    ahead = over_groups(down_sums + up_sums, None)
    grad_normalized = grad_resid_two + reduce_core(dot(grad_upward, up_full, turned))
    grad_resid_one, grad_gain_one, grad_shift_one = normalize_back(
        grad_normalized, first_standardized, first_inverse, gain_one
    )
    grad_out_bias = jnp.sum(grad_resid_one, axis=0)
    grad_attn_all = gather_core(grad_resid_one.astype(BF16))
    out_sums = plane_sums(dot(context, grad_attn_all, across), column_blocks)
    grad_context = dot(grad_attn_all, out_full, turned).astype(BF16)
    grad_mixed = attend_back(mixed, grad_context, log_sums, place)
    qkv_sums = plane_sums(dot(tokens_all, grad_mixed, across), row_blocks)
    grad_tokens = hand_back(grad_resid_one + reduce_core(dot(grad_mixed, qkv_full, turned)))

    def row_wide(values):
        blocks = values.reshape(2, 2, width)
        return turn(blocks, x, 0).reshape(-1)

    def col_wide(values):
        blocks = values.reshape(2, 1, -1)
        blocks = turn(blocks, col, 0)
        zeros = jnp.zeros_like(blocks)
        return in_order(core, blocks, zeros, 1).reshape(-1)

    row_list = [
        grad_out_bias,
        grad_gain_one,
        grad_shift_one,
        grad_down_bias,
        grad_gain_two,
        grad_shift_two,
    ]
    head_sums = jnp.sum(grad_mixed, axis=0, dtype=F32).reshape(-1, 3, HD)

    def plane_total(parts):
        total = jnp.concatenate(parts)
        for axis in ("core", "x", "col"):
            total = total + swap(total, axis)
        return total

    early = plane_total([row_wide(values) for values in row_list] + [col_wide(grad_up_bias)])
    late = plane_total(
        [col_wide(head_sums[:, 0].reshape(-1)), col_wide(head_sums[:, 2].reshape(-1))]
    )
    down_first, down_second, up_first, up_second = ahead
    out_first, out_second, qkv_first, qkv_second, early, late = over_groups(
        out_sums + qkv_sums + (early, late), ahead
    )
    early = early.astype(F32)
    late = late.astype(F32).reshape(2, -1)
    grad_down_weight = settle(down_first, down_second, 0)
    grad_up_weight = settle(up_first, up_second, 1)
    grad_out_weight = settle(out_first, out_second, 0)
    grad_qkv_weight = settle(qkv_first, qkv_second, 1)
    row_sums = [
        lax.dynamic_slice_in_dim(
            early, index * 4 * width + (2 * x + core) * width, width, 0
        )
        for index in range(count)
    ]
    up_sum = lax.dynamic_slice_in_dim(early, count * 4 * width + col * up_amount, up_amount, 0)
    late = lax.dynamic_slice_in_dim(late, col * head_amount, head_amount, 1)
    return (
        layer_result_output,
        grad_tokens,
        grad_qkv_weight,
        late[0],
        late[1],
        grad_out_weight,
        row_sums[0],
        row_sums[1],
        row_sums[2],
        grad_up_weight,
        up_sum,
        grad_down_weight,
        row_sums[3],
        row_sums[4],
        row_sums[5],
    )


def solution(mesh):
    sizes = mesh.shape
    fine = Mesh(
        mesh.devices.reshape(sizes["dp"], sizes["row"] // 2, 2, sizes["col"]),
        ("dp", "x", "core", "col"),
    )
    row = ("x", "core")
    activation = P(("dp", "col"), row)
    return jax.shard_map(
        shards,
        mesh=fine,
        in_specs=(
            activation,
            P("dp"),
            P(row, "col"),
            P("col"),
            P("col"),
            P("col", row),
            P(row),
            P(row),
            P(row),
            P(row, "col"),
            P("col"),
            P("col", row),
            P(row),
            P(row),
            P(row),
            activation,
        ),
        out_specs=(
            activation,
            activation,
            P(row, "col"),
            P("col"),
            P("col"),
            P("col", row),
            P(row),
            P(row),
            P(row),
            P(row, "col"),
            P("col"),
            P("col", row),
            P(row),
            P(row),
            P(row),
        ),
        check_vma=False,
    )
```
